32 devices in a mesh: dp: 16 (over z, x, core), seq: 2 (over y).
Axes of the slice: x: 2, y: 2, z: 4, core: 2. Of those that a mesh axis runs over, the one named last changes fastest.
Arguments:
- tokens: bfloat16 [16, 384, 768], P('dp', 'seq'), may hold values from -6 to 6
- segment_ids: int32 [16, 384], P('dp'), may hold values from 0 to 383, as said below
- buckets: int32 [384], replicated, may hold values from 0 to 31, as said below
- encoder: bfloat16 [16, 256, 768], P('dp', 'seq'), may hold values from -6 to 6
- norm_gains: float32 [3, 768], replicated, may hold values from 0.1 to 1.9
- rel_table: float32 [32, 12], replicated, may hold values from -4 to 4
- attn_in: bfloat16 [768, 2304], P(('dp', 'seq')), may hold values from -0.109375 to 0.109375
- attn_out: bfloat16 [768, 768], P(('dp', 'seq')), may hold values from -0.875 to 0.875
- cross_query: bfloat16 [768, 768], P(('dp', 'seq')), may hold values from -0.109375 to 0.109375
- cross_kv: bfloat16 [768, 1536], P(('dp', 'seq')), may hold values from -0.109375 to 0.109375
- cross_out: bfloat16 [768, 768], P(('dp', 'seq')), may hold values from -0.875 to 0.875
- ff_in: bfloat16 [768, 4096], P(('dp', 'seq')), may hold values from -0.21875 to 0.21875
- ff_out: bfloat16 [768, 2048], P(('dp', 'seq')), may hold values from -0.125 to 0.125
- cotangent: bfloat16 [16, 384, 768], P('dp', 'seq'), may hold values from -6 to 6
Outputs:
- block_out: bfloat16 [16, 384, 768], P('dp', 'seq')
- tokens_grad: float32 [16, 384, 768], P('dp', 'seq')
- encoder_grad: float32 [16, 256, 768], P('dp', 'seq')
- norm_gains_grad: float32 [3, 768], replicated
- rel_table_grad: float32 [32, 12], replicated
- attn_in_grad: float32 [768, 2304], P(('dp', 'seq'))
- attn_out_grad: float32 [768, 768], P(('dp', 'seq'))
- cross_query_grad: float32 [768, 768], P(('dp', 'seq'))
- cross_kv_grad: float32 [768, 1536], P(('dp', 'seq'))
- cross_out_grad: float32 [768, 768], P(('dp', 'seq'))
- ff_in_grad: float32 [768, 4096], P(('dp', 'seq'))
- ff_out_grad: float32 [768, 2048], P(('dp', 'seq'))
The draws below stay inside these ranges and needn't reach their ends.
Inputs may be any that keep to these rules, and one draw needn't show every extreme that they name: `segment_ids`: non-decreasing along each sequence; each position holds the first position of its document; documents start only at position 0, at positions 1 to 96, or after 3 * 96, so one document covers positions 96 to 288; the last position always starts a document of its own. `buckets`: non-decreasing in the distance, 0 at distance 0 and 31 at distance 384 - 1.
All inputs are finite; a program needn't handle non-finite values.
Results may differ from the reference program's by a relative error of at most 0.024.
The reference program's roundings to bfloat16 on the way count: a program that leaves them out, or rounds other values in their place, can miss the bound.
Values may be sent and summed in bfloat16 or wider, within the bound.
A program may use at most 256 MiB of HBM per device.

```python
import jax
import jax.numpy as jnp
from jax import lax

D = 768
H = 12
HD = 64
FF = 2048
NB = 32
SEQS = 16
LENGTH = 384
ENC = 256


def draw_segment_ids(key, part):
    key = jax.random.fold_in(key, 11)
    coins = jax.random.randint(key, (SEQS, LENGTH), 0, 16)
    position = jnp.arange(LENGTH, dtype=jnp.int32)
    outer = (position >= 1) & (position <= LENGTH // 4) | (position > 3 * LENGTH // 4)
    starts = (coins == 0) & outer[None, :] | (position[None, :] == LENGTH - 1)
    first_pos = jnp.where(starts, position[None, :], 0).astype(jnp.int32)
    return lax.cummax(first_pos, axis=1).astype(jnp.int32)


def draw_buckets(key, part):
    key = jax.random.fold_in(key, 23)
    breaks = jax.random.permutation(key, LENGTH - 1)[:NB - 1].astype(jnp.int32) + 1
    position = jnp.arange(LENGTH, dtype=jnp.int32)
    return jnp.sum((breaks[None, :] <= position[:, None]).astype(jnp.int32), axis=1).astype(jnp.int32)


def with_spikes(values, key, source, target, shards_of, factor):
    def block_of(dim):
        return (jnp.arange(values.shape[dim]) // (values.shape[dim] // shards_of)).reshape((-1,) + (1,) * (values.ndim - 1 - dim))

    one_side = jax.random.permutation(key, shards_of)[block_of(target)]
    far = (block_of(target) + shards_of // 2) % shards_of
    return jnp.where((block_of(source) == one_side) | (block_of(source) == far), factor * values, values)


def steps_of(key, extent, split, smallest, top_value):
    loudness, own = 1.0, jax.random.fold_in(key, 6)
    for axis_at, blocks in split:
        steps = jnp.exp(jax.random.uniform(jax.random.fold_in(own, axis_at), (blocks,), jnp.float32, smallest / len(split), top_value / len(split)))
        loudness = loudness * jnp.repeat(steps, extent[axis_at] // blocks).reshape([-1 if axis == axis_at else 1 for axis in range(len(extent))])
    return loudness


def normal_values(stream_key, shape, deviation, bound, split=(), kind=jnp.bfloat16):
    values = jax.random.normal(stream_key, shape, jnp.float32) * deviation
    if len(split) > 0:
        values = steps_of(stream_key, shape, split, -0.22, 0.18) * values
    return jnp.clip(values, min=-bound, max=bound).astype(kind)


def bell_draw_with(stream_key, shape, width, reach, cuts, heavy, held_as=jnp.bfloat16):
    drawn = width * jax.random.normal(stream_key, shape, jnp.float32)
    if cuts:
        drawn = drawn * steps_of(stream_key, shape, cuts, -0.22, 0.18)
    return jnp.clip(with_spikes(drawn, jax.random.fold_in(stream_key, 3), *heavy), -reach, reach).astype(held_as)


def setup_inputs(seed: int = 0) -> dict:
    key_list = jax.random.split(jax.random.key(seed), 15)
    tokens = normal_values(key_list[0], (SEQS, LENGTH, D), 1.0, 6.0, ((0, 16), (1, 2)))
    segment_ids = draw_segment_ids(jax.random.fold_in(key_list[14], 71), 0)
    buckets = draw_buckets(jax.random.fold_in(key_list[14], 71), 0)
    encoder = normal_values(key_list[3], (SEQS, ENC, D), 1.0, 6.0, ((0, 16), (1, 2)))
    norm_gains = jnp.clip(1.0 + 0.18 * jax.random.normal(key_list[4], (3, D), jnp.float32), 0.1, 1.9)
    rel_table = normal_values(key_list[5], (NB, H), 1.0, 4.0, (), jnp.float32)
    attn_in = normal_values(key_list[6], (D, 3 * D), (4 * D) ** -0.5, 0.109375, ((0, 32),))
    attn_out = normal_values(key_list[7], (D, D), (D // 16) ** -0.5, 0.875, ((0, 32),))
    cross_query = normal_values(key_list[8], (D, D), (4 * D) ** -0.5, 0.109375, ((0, 32),))
    cross_kv = normal_values(key_list[9], (D, 2 * D), (4 * D) ** -0.5, 0.109375, ((0, 32),))
    cross_out = normal_values(key_list[10], (D, D), (D // 16) ** -0.5, 0.875, ((0, 32),))
    ff_in = normal_values(key_list[11], (D, 2 * FF), D ** -0.5, 0.21875, ((0, 32),))
    ff_out = normal_values(key_list[12], (D, FF), FF ** -0.5, 0.125, ((0, 32),))
    cotangent = bell_draw_with(key_list[13], (SEQS, LENGTH, D), 1.0, 6.0, ((0, 16), (1, 2)), (0, 2, 16, 2.0))
    return {"tokens": tokens, "segment_ids": segment_ids, "buckets": buckets, "encoder": encoder, "norm_gains": norm_gains, "rel_table": rel_table, "attn_in": attn_in, "attn_out": attn_out, "cross_query": cross_query, "cross_kv": cross_kv, "cross_out": cross_out, "ff_in": ff_in, "ff_out": ff_out, "cotangent": cotangent}


@jax.custom_vjp
def low(v):
    return lax.optimization_barrier(v.astype(jnp.bfloat16)).astype(jnp.float32)

@jax.custom_vjp
def low_back(v):
    return v

def low_keep(v):
    return (low(v), None)

def low_pass(kept, grad):
    return (grad,)

def back_keep(v):
    return (v, None)

def back_low(kept, grad):
    return (low(grad),)
low.defvjp(low_keep, low_pass)
low_back.defvjp(back_keep, back_low)
epsilon = 1e-06
masked_value = -1000000000.0

def rms_scaled(values, gain_row):
    return values * lax.rsqrt(lax.optimization_barrier(jnp.mean(values * values, axis=-1, keepdims=True)) + epsilon) * gain_row

def gelu_tanh(values):
    return 0.5 * values * (1.0 + jnp.tanh(0.7978845608028654 * (values + 0.044715 * values * values * values)))

def softmax_rows(scores):
    row_top = lax.optimization_barrier(jnp.max(scores, axis=-1, keepdims=True))
    exponent = jnp.exp(scores - row_top)
    return exponent / lax.optimization_barrier(jnp.sum(exponent, axis=-1, keepdims=True))

def split_heads(values):
    return values.reshape(values.shape[0], H, HD)

def attention(queries, key_rows, values, rel_bias, allowed):
    highest = lax.Precision.HIGHEST
    scores = jnp.einsum('qhd,khd->hqk', split_heads(queries), split_heads(key_rows), precision=highest)
    if rel_bias is not None:
        scores = jnp.where(allowed[None], scores + rel_bias, masked_value)
    scores = low_back(scores)
    att_probs = low(softmax_rows(scores))
    context = jnp.einsum('hqk,khd->qhd', att_probs, split_heads(values), precision=highest)
    return low_back(low(context.reshape(queries.shape[0], -1)))

def layer(tokens, encoder, norm_gains, rel_table, matrices, allowed, bucket_grid):
    attn_in, attn_out, cross_query, cross_kv, cross_out, ff_in, ff_out = matrices
    highest = lax.Precision.HIGHEST
    model_width = tokens.shape[1]
    normed = low(rms_scaled(tokens, norm_gains[0]))
    qkv_rows = low_back(low(jnp.dot(normed, attn_in, precision=highest)))
    rel_bias = jnp.take(rel_table, bucket_grid, axis=0).transpose(2, 0, 1)
    context = attention(qkv_rows[:, :model_width], qkv_rows[:, model_width:2 * model_width], qkv_rows[:, 2 * model_width:], rel_bias, allowed)
    hidden_one = tokens + low_back(jnp.dot(context, attn_out, precision=highest))
    normed = low(rms_scaled(hidden_one, norm_gains[1]))
    query_two = low_back(low(jnp.dot(normed, cross_query, precision=highest)))
    keyval_two = low_back(low(jnp.dot(encoder, cross_kv, precision=highest)))
    context = attention(query_two, keyval_two[:, :model_width], keyval_two[:, model_width:], None, None)
    hidden_two = hidden_one + low_back(jnp.dot(context, cross_out, precision=highest))
    normed = low(rms_scaled(hidden_two, norm_gains[2]))
    pre_act = low_back(jnp.dot(normed, ff_in, precision=highest))
    mixed_act = low(gelu_tanh(pre_act[:, :FF]) * pre_act[:, FF:])
    return hidden_two + low_back(jnp.dot(mixed_act, ff_out.T, precision=highest))

def reference(tokens, segment_ids, buckets, encoder, norm_gains, rel_table, attn_in, attn_out, cross_query, cross_kv, cross_out, ff_in, ff_out, cotangent):
    matrices = tuple((mat.astype(jnp.float32) for mat in (attn_in, attn_out, cross_query, cross_kv, cross_out, ff_in, ff_out)))
    position = jnp.arange(LENGTH, dtype=jnp.int32)
    distance = jnp.maximum(position[:, None] - position[None, :], 0)
    bucket_grid = jnp.take(buckets, distance, axis=0)
    causal = position[None, :] <= position[:, None]

    def one_sequence(totals, row):
        tok_row, enc_row, seg_row, cot_row = row
        allowed = causal & (seg_row[:, None] == seg_row[None, :])

        def forward(tok_in, enc_in, gain_in, table_in, mats_in):
            return layer(tok_in, enc_in, gain_in, table_in, mats_in, allowed, bucket_grid)
        result, pullback = jax.vjp(forward, tok_row, enc_row, norm_gains, rel_table, matrices)
        grads = pullback(cot_row)
        fresh = (grads[2], grads[3]) + tuple(grads[4])
        totals = tuple((acc + part_grad for acc, part_grad in zip(totals, fresh)))
        return (totals, (result.astype(jnp.bfloat16), grads[0], grads[1]))
    init = tuple((jnp.zeros_like(arr) for arr in (norm_gains, rel_table) + matrices))
    totals, outputs = lax.scan(one_sequence, init, (tokens.astype(jnp.float32), encoder.astype(jnp.float32), segment_ids, cotangent.astype(jnp.float32)))
    return (outputs[0], outputs[1], outputs[2], totals[0], totals[1], totals[2], totals[3], totals[4], totals[5], totals[6], totals[7], totals[8])
```

```python
import functools

import jax
import jax.numpy as jnp
from jax import lax
from jax.sharding import PartitionSpec as P

H = 12
HD = 64
FF = 2048


epsilon = 1e-06
masked_value = -1000000000.0


def rms_scaled(values, gain_row):
    return (
        values * lax.rsqrt(jnp.mean(values * values, axis=-1, keepdims=True) + epsilon) * gain_row
    )


def gelu_tanh(values):
    return (
        0.5
        * values
        * (1.0 + jnp.tanh(0.7978845608028654 * (values + 0.044715 * values * values * values)))
    )


def gated(gate_act, upward):
    return gelu_tanh(gate_act) * upward


def bias_table(table_in, grid_onehot):
    return jnp.einsum("bij,bh->hij", grid_onehot, table_in, precision=lax.Precision.HIGHEST)


def attend_forward(queries, key_rows, values, rel_bias, allowed):
    scores = jnp.einsum("rhd,shd->hrs", queries, key_rows, preferred_element_type=jnp.float32)
    if rel_bias is not None:
        scores = jnp.where(allowed[None], scores + rel_bias, masked_value)
    row_top = jnp.max(scores, axis=2, keepdims=True)
    exponent = jnp.exp(scores - row_top)
    row_total = jnp.sum(exponent, axis=2, keepdims=True)
    weights_full = exponent / row_total
    context = jnp.einsum(
        "hrs,shd->rhd",
        weights_full.astype(jnp.bfloat16),
        values,
        preferred_element_type=jnp.float32,
    )
    return (context.astype(jnp.bfloat16), weights_full)


def attend_backward(queries, key_rows, values, weights_full, grad_context):
    weights_low = weights_full.astype(jnp.bfloat16)
    grad_values = jnp.einsum(
        "hrs,rhd->shd", weights_low, grad_context, preferred_element_type=jnp.float32
    )
    grad_weights = jnp.einsum(
        "rhd,shd->hrs", grad_context, values, preferred_element_type=jnp.float32
    )
    row_dot = jnp.sum(grad_weights * weights_full, axis=2, keepdims=True)
    grad_scores = (weights_full * (grad_weights - row_dot)).astype(jnp.bfloat16)
    grad_queries = jnp.einsum(
        "hrs,shd->rhd", grad_scores, key_rows, preferred_element_type=jnp.float32
    )
    grad_keys = jnp.einsum("hrs,rhd->shd", grad_scores, queries, preferred_element_type=jnp.float32)
    return (grad_queries, grad_keys, grad_values, grad_scores)


def outer_rows(left, right):
    return jnp.einsum("tc,tk->ck", left, right, preferred_element_type=jnp.float32).astype(
        jnp.bfloat16
    )


axes = ("dp", "seq")


def swap_bit(values, bit, devices):
    return lax.ppermute(values, axes, [(at, at ^ (1 << bit)) for at in range(devices)])


def bit_order(bits, turn):
    rest = [0] + list(range(2, bits))
    turn = turn % len(rest)
    return [1] + rest[turn:] + rest[:turn]


def scatter_sum(values, order, devices, index):
    bits = len(order)
    values = values.reshape((2,) * bits + (values.shape[0] // devices, values.shape[1]))
    left = list(range(bits - 1, -1, -1))
    for bit in order:
        place = left.index(bit)
        mine = (index >> bit) & 1
        kept = lax.dynamic_index_in_dim(values, mine, place, keepdims=False)
        sent = lax.dynamic_index_in_dim(values, 1 - mine, place, keepdims=False)
        total = kept.astype(jnp.float32) + swap_bit(sent, bit, devices).astype(jnp.float32)
        left.remove(bit)
        values = total.astype(jnp.bfloat16) if left else total
    return values


def full_sum(values, bits, devices):
    for bit in range(bits):
        values = values + swap_bit(values, bit, devices)
    return values


def local(
    devices,
    tokens,
    segment_ids,
    buckets,
    encoder,
    norm_gains,
    rel_table,
    attn_in,
    attn_out,
    cross_query,
    cross_kv,
    cross_out,
    ff_in,
    ff_out,
    cotangent,
):
    bits = devices.bit_length() - 1
    tok_count = tokens.shape[1]
    model_width = tokens.shape[2]
    enc_count = encoder.shape[1]
    my_seq = lax.axis_index("seq")
    index = lax.axis_index("dp") * 2 + my_seq

    def scattered(values, turn):
        return scatter_sum(values, bit_order(bits, turn), devices, index)

    shards = (attn_in, attn_out, cross_query, cross_kv, cross_out, ff_in, ff_out)
    gathered = lax.all_gather(jnp.concatenate(shards, 1), axes, axis=0, tiled=True)
    whole = []
    column = 0
    for shard in shards:
        whole.append(gathered[:, column : column + shard.shape[1]])
        column += shard.shape[1]
    (
        attn_in_all,
        attn_out_all,
        cross_query_all,
        cross_kv_all,
        cross_out_all,
        ff_in_all,
        ff_out_all,
    ) = whole

    tokens_both = jnp.concatenate([tokens[0], swap_bit(tokens[0], 0, devices)], 0)
    enc_both = jnp.concatenate([encoder[0], swap_bit(encoder[0], 0, devices)], 0)
    tok_float = tokens[0].astype(jnp.float32)
    segments = segment_ids[0]
    own_start = my_seq * tok_count
    other_start = (1 - my_seq) * tok_count
    steps = jnp.arange(tok_count, dtype=jnp.int32)
    query_pos = own_start + steps
    key_pos = jnp.concatenate([query_pos, other_start + steps])
    query_seg = lax.dynamic_slice_in_dim(segments, own_start, tok_count)
    key_seg = jnp.concatenate(
        [query_seg, lax.dynamic_slice_in_dim(segments, other_start, tok_count)]
    )
    allowed = (key_pos[None, :] <= query_pos[:, None]) & (query_seg[:, None] == key_seg[None, :])
    distance = jnp.maximum(query_pos[:, None] - key_pos[None, :], 0)
    bucket_ids = jnp.arange(rel_table.shape[0], dtype=jnp.int32)
    range_from = jnp.sum((buckets[None, :] < bucket_ids[:, None]).astype(jnp.int32), axis=1)
    range_to = jnp.sum((buckets[None, :] <= bucket_ids[:, None]).astype(jnp.int32), axis=1)
    grid_onehot = (
        (distance[None] >= range_from[:, None, None]) & (distance[None] < range_to[:, None, None])
    ).astype(jnp.float32)
    rel_bias = bias_table(rel_table, grid_onehot)

    normed_both = rms_scaled(tokens_both.astype(jnp.float32), norm_gains[0]).astype(jnp.bfloat16)
    qkv_both = jnp.dot(normed_both, attn_in_all, preferred_element_type=jnp.float32).astype(
        jnp.bfloat16
    )
    queries_one = qkv_both[:tok_count, :model_width].reshape(tok_count, H, HD)
    keys_one = qkv_both[:, model_width : 2 * model_width].reshape(2 * tok_count, H, HD)
    values_one = qkv_both[:, 2 * model_width :].reshape(2 * tok_count, H, HD)
    context, weights_one = attend_forward(queries_one, keys_one, values_one, rel_bias, allowed)
    context_one = context.reshape(tok_count, model_width)
    hidden_one = tok_float + jnp.dot(context_one, attn_out_all, preferred_element_type=jnp.float32)
    normed_two = rms_scaled(hidden_one, norm_gains[1]).astype(jnp.bfloat16)
    queries_two = (
        jnp.dot(normed_two, cross_query_all, preferred_element_type=jnp.float32)
        .astype(jnp.bfloat16)
        .reshape(tok_count, H, HD)
    )
    keyval_two = jnp.dot(enc_both, cross_kv_all, preferred_element_type=jnp.float32).astype(
        jnp.bfloat16
    )
    keys_two = keyval_two[:, :model_width].reshape(2 * enc_count, H, HD)
    values_two = keyval_two[:, model_width:].reshape(2 * enc_count, H, HD)
    context, weights_two = attend_forward(queries_two, keys_two, values_two, None, None)
    context_two = context.reshape(tok_count, model_width)
    hidden_two = hidden_one + jnp.dot(
        context_two, cross_out_all, preferred_element_type=jnp.float32
    )
    normed_three = rms_scaled(hidden_two, norm_gains[2]).astype(jnp.bfloat16)
    pre_act = jnp.dot(normed_three, ff_in_all, preferred_element_type=jnp.float32)
    gate_act = pre_act[:, :FF]
    upward = pre_act[:, FF:]
    mixed_act = gated(gate_act, upward).astype(jnp.bfloat16)
    layer_out = hidden_two + jnp.einsum(
        "tf,df->td", mixed_act, ff_out_all, preferred_element_type=jnp.float32
    )
    grad_out = cotangent[0].astype(jnp.float32)
    grad_branch = cotangent[0]
    ff_out_grad = scattered(outer_rows(grad_branch, mixed_act), 0)
    grad_mixed = jnp.einsum(
        "td,df->tf", grad_branch, ff_out_all, preferred_element_type=jnp.float32
    )
    gate_value, gate_pull = jax.vjp(gated, gate_act, upward)
    grad_gate, grad_up = gate_pull(grad_mixed)
    grad_gate = grad_gate.astype(jnp.bfloat16)
    grad_up = grad_up.astype(jnp.bfloat16)
    gate_grad = scattered(outer_rows(normed_three, grad_gate), 1)
    up_grad = scattered(outer_rows(normed_three, grad_up), 2)
    grad_pre = jnp.concatenate([grad_gate, grad_up], 1)
    grad_normed = jnp.einsum("tk,ck->tc", grad_pre, ff_in_all, preferred_element_type=jnp.float32)
    norm_value, norm_pull = jax.vjp(rms_scaled, hidden_two, norm_gains[2])
    grad_resid, gain_three = norm_pull(grad_normed)
    grad_hidden_two = grad_out + grad_resid
    grad_branch_two = grad_hidden_two.astype(jnp.bfloat16)
    grad_context_two = jnp.einsum(
        "tk,ck->tc", grad_branch_two, cross_out_all, preferred_element_type=jnp.float32
    )
    grad_context_two = grad_context_two.astype(jnp.bfloat16).reshape(tok_count, H, HD)
    grad_queries, grad_keys, grad_values, grad_scores = attend_backward(
        queries_two, keys_two, values_two, weights_two, grad_context_two
    )
    grad_kv_two = jnp.concatenate(
        [
            grad_keys.reshape(2 * enc_count, model_width),
            grad_values.reshape(2 * enc_count, model_width),
        ],
        1,
    )
    kv_two_low = grad_kv_two.astype(jnp.bfloat16)
    cross_grads = scattered(
        jnp.concatenate(
            [outer_rows(enc_both, kv_two_low), outer_rows(context_two, grad_branch_two)], 1
        ),
        1,
    )
    grad_kv_local = (
        grad_kv_two[:enc_count]
        + swap_bit(kv_two_low[enc_count:], 0, devices).astype(jnp.float32)
    ).astype(jnp.bfloat16)
    grad_queries_two = grad_queries.reshape(tok_count, model_width).astype(jnp.bfloat16)
    encoder_grad = jnp.einsum(
        "tk,ck->tc", grad_kv_local, cross_kv_all, preferred_element_type=jnp.float32
    )
    grad_normed = jnp.einsum(
        "tk,ck->tc", grad_queries_two, cross_query_all, preferred_element_type=jnp.float32
    )
    norm_value, norm_pull = jax.vjp(rms_scaled, hidden_one, norm_gains[1])
    grad_resid, gain_two = norm_pull(grad_normed)
    grad_hidden_one = grad_hidden_two + grad_resid
    grad_branch_one = grad_hidden_one.astype(jnp.bfloat16)
    middle_grads = scattered(
        jnp.concatenate(
            [outer_rows(normed_two, grad_queries_two), outer_rows(context_one, grad_branch_one)], 1
        ),
        2,
    )
    grad_context_one = jnp.einsum(
        "tk,ck->tc", grad_branch_one, attn_out_all, preferred_element_type=jnp.float32
    )
    grad_context_one = grad_context_one.astype(jnp.bfloat16).reshape(tok_count, H, HD)
    grad_queries, grad_keys, grad_values, grad_scores = attend_backward(
        queries_one, keys_one, values_one, weights_one, grad_context_one
    )
    grad_keys = grad_keys.reshape(2 * tok_count, model_width)
    grad_values = grad_values.reshape(2 * tok_count, model_width)
    keys_low = grad_keys.astype(jnp.bfloat16)
    values_low = grad_values.astype(jnp.bfloat16)
    grad_queries_one = grad_queries.reshape(tok_count, model_width).astype(jnp.bfloat16)
    in_grads = [
        scattered(outer_rows(normed_both, values_low), 0),
        scattered(outer_rows(normed_both, keys_low), 1),
        scattered(outer_rows(normed_both[:tok_count], grad_queries_one), 2),
    ]
    other_part = swap_bit(
        jnp.concatenate([keys_low[tok_count:], values_low[tok_count:]], 1), 0, devices
    ).astype(jnp.float32)
    grad_kv_own = (
        jnp.concatenate([grad_keys[:tok_count], grad_values[:tok_count]], 1) + other_part
    ).astype(jnp.bfloat16)
    table_grad = jnp.einsum(
        "hij,bij->bh", grad_scores.astype(jnp.float32), grid_onehot, precision=lax.Precision.HIGHEST
    )
    grad_qkv = jnp.concatenate([grad_queries_one, grad_kv_own], 1)
    grad_normed = jnp.einsum("tk,ck->tc", grad_qkv, attn_in_all, preferred_element_type=jnp.float32)
    norm_value, norm_pull = jax.vjp(rms_scaled, tok_float, norm_gains[0])
    grad_resid, gain_one = norm_pull(grad_normed)
    tokens_grad = grad_hidden_one + grad_resid
    small = jnp.concatenate([gain_one, gain_two, gain_three, table_grad.reshape(-1)])
    small = full_sum(small, bits, devices)
    return (
        layer_out.astype(jnp.bfloat16)[None],
        tokens_grad[None],
        encoder_grad[None],
        small[: 3 * model_width].reshape(3, model_width),
        small[3 * model_width :].reshape(rel_table.shape),
        jnp.concatenate([in_grads[2], in_grads[1], in_grads[0]], 1),
        middle_grads[:, model_width:],
        middle_grads[:, :model_width],
        cross_grads[:, : 2 * model_width],
        cross_grads[:, 2 * model_width :],
        jnp.concatenate([gate_grad, up_grad], 1),
        ff_out_grad,
    )


def solution(mesh):
    return jax.shard_map(
        functools.partial(local, mesh.devices.size),
        mesh=mesh,
        in_specs=(
            P("dp", "seq", None),
            P("dp", None),
            P(),
            P("dp", "seq", None),
            P(),
            P(),
            P(("dp", "seq"), None),
            P(("dp", "seq"), None),
            P(("dp", "seq"), None),
            P(("dp", "seq"), None),
            P(("dp", "seq"), None),
            P(("dp", "seq"), None),
            P(("dp", "seq"), None),
            P("dp", "seq", None),
        ),
        out_specs=(
            P("dp", "seq", None),
            P("dp", "seq", None),
            P("dp", "seq", None),
            P(),
            P(),
            P(("dp", "seq"), None),
            P(("dp", "seq"), None),
            P(("dp", "seq"), None),
            P(("dp", "seq"), None),
            P(("dp", "seq"), None),
            P(("dp", "seq"), None),
            P(("dp", "seq"), None),
        ),
        check_vma=False,
    )
```

```python
import functools

import jax
import jax.numpy as jnp
from jax import lax
from jax.sharding import PartitionSpec as P

H = 12
HD = 64
FF = 2048


epsilon = 1e-06
masked_value = -1000000000.0


def rms_scaled(values, gain_row):
    return (
        values * lax.rsqrt(jnp.mean(values * values, axis=-1, keepdims=True) + epsilon) * gain_row
    )


def gelu_tanh(values):
    return (
        0.5
        * values
        * (1.0 + jnp.tanh(0.7978845608028654 * (values + 0.044715 * values * values * values)))
    )


def gated(gate_act, upward):
    return gelu_tanh(gate_act) * upward


def bias_table(table_in, grid_onehot):
    return jnp.einsum("bij,bh->hij", grid_onehot, table_in, precision=lax.Precision.HIGHEST)


def attend_forward(queries, key_rows, values, rel_bias, allowed):
    scores = jnp.einsum("rhd,shd->hrs", queries, key_rows, preferred_element_type=jnp.float32)
    if rel_bias is not None:
        scores = jnp.where(allowed[None], scores + rel_bias, masked_value)
    row_top = jnp.max(scores, axis=2, keepdims=True)
    exponent = jnp.exp(scores - row_top)
    row_total = jnp.sum(exponent, axis=2, keepdims=True)
    weights_full = exponent / row_total
    context = jnp.einsum(
        "hrs,shd->rhd",
        weights_full.astype(jnp.bfloat16),
        values,
        preferred_element_type=jnp.float32,
    )
    return (context.astype(jnp.bfloat16), weights_full)


def attend_backward(queries, key_rows, values, weights_full, grad_context):
    weights_low = weights_full.astype(jnp.bfloat16)
    grad_values = jnp.einsum(
        "hrs,rhd->shd", weights_low, grad_context, preferred_element_type=jnp.float32
    )
    grad_weights = jnp.einsum(
        "rhd,shd->hrs", grad_context, values, preferred_element_type=jnp.float32
    )
    row_dot = jnp.sum(grad_weights * weights_full, axis=2, keepdims=True)
    grad_scores = (weights_full * (grad_weights - row_dot)).astype(jnp.bfloat16)
    grad_queries = jnp.einsum(
        "hrs,shd->rhd", grad_scores, key_rows, preferred_element_type=jnp.float32
    )
    grad_keys = jnp.einsum("hrs,rhd->shd", grad_scores, queries, preferred_element_type=jnp.float32)
    return (grad_queries, grad_keys, grad_values, grad_scores)


def outer_rows(left, right):
    return jnp.einsum("tc,tk->ck", left, right, preferred_element_type=jnp.float32).astype(
        jnp.bfloat16
    )


axes = ("dp", "seq")


def swap_bit(values, bit, devices):
    return lax.ppermute(values, axes, [(at, at ^ (1 << bit)) for at in range(devices)])


def bit_order(bits, turn):
    rest = [0] + list(range(2, bits))
    turn = turn % len(rest)
    return [1] + rest[turn:] + rest[:turn]


def after(never, values, others):
    first = [other[(0,) * other.ndim].astype(jnp.float32) for other in others]
    return jnp.where(never, sum(first).astype(values.dtype), values)


class HalvingSum:

    def __init__(self, groups, devices, index, never, whole=None):
        self.devices, self.index, self.never, self.whole = devices, index, never, whole
        self.bits = devices.bit_length() - 1
        self.at = 0
        self.orders = [bit_order(self.bits, turn) for turn in range(len(groups))]
        self.left = [list(range(self.bits - 1, -1, -1)) for group in groups]
        self.groups = [
            group.reshape((2,) * self.bits + (group.shape[0] // devices, group.shape[1]))
            for group in groups
        ]
        self.sent = self.halves(1)

    def halves(self, other):
        found = []
        for order, left, group in zip(self.orders, self.left, self.groups):
            bit = order[self.at]
            mine = ((self.index >> bit) & 1) ^ other
            found.append(
                lax.dynamic_index_in_dim(group, mine, left.index(bit), keepdims=False)
            )
        return found

    def exchange(self):
        kept = self.halves(0)
        last = self.at == self.bits - 1
        came = []
        for order, left, sent in zip(self.orders, self.left, self.sent):
            left.remove(order[self.at])
            came.append(swap_bit(sent, order[self.at], self.devices))
        if self.whole is not None:
            self.whole = self.whole + swap_bit(
                after(self.never, self.whole, self.sent[:1]), self.at, self.devices
            )
        totals = [one.astype(jnp.float32) + two.astype(jnp.float32) for one, two in zip(kept, came)]
        self.at += 1
        if last:
            self.groups = totals
            return
        self.groups = [total.astype(jnp.bfloat16) for total in totals]
        marks = came + ([] if self.whole is None else [self.whole])
        self.sent = [after(self.never, sent, marks) for sent in self.halves(1)]


def local(
    devices,
    tokens,
    segment_ids,
    buckets,
    encoder,
    norm_gains,
    rel_table,
    attn_in,
    attn_out,
    cross_query,
    cross_kv,
    cross_out,
    ff_in,
    ff_out,
    cotangent,
):
    bits = devices.bit_length() - 1
    tok_count = tokens.shape[1]
    model_width = tokens.shape[2]
    enc_count = encoder.shape[1]
    my_seq = lax.axis_index("seq")
    index = lax.axis_index("dp") * 2 + my_seq

    never = segment_ids[0, 0] < 0

    shards = (attn_in, attn_out, cross_query, cross_kv, cross_out, ff_in, ff_out)
    gathered = lax.all_gather(jnp.concatenate(shards, 1), axes, axis=0, tiled=True)
    whole = []
    column = 0
    for shard in shards:
        whole.append(gathered[:, column : column + shard.shape[1]])
        column += shard.shape[1]
    (
        attn_in_all,
        attn_out_all,
        cross_query_all,
        cross_kv_all,
        cross_out_all,
        ff_in_all,
        ff_out_all,
    ) = whole

    tokens_both = jnp.concatenate([tokens[0], swap_bit(tokens[0], 0, devices)], 0)
    enc_both = jnp.concatenate([encoder[0], swap_bit(encoder[0], 0, devices)], 0)
    tok_float = tokens[0].astype(jnp.float32)
    segments = segment_ids[0]
    own_start = my_seq * tok_count
    other_start = (1 - my_seq) * tok_count
    steps = jnp.arange(tok_count, dtype=jnp.int32)
    query_pos = own_start + steps
    key_pos = jnp.concatenate([query_pos, other_start + steps])
    query_seg = lax.dynamic_slice_in_dim(segments, own_start, tok_count)
    key_seg = jnp.concatenate(
        [query_seg, lax.dynamic_slice_in_dim(segments, other_start, tok_count)]
    )
    allowed = (key_pos[None, :] <= query_pos[:, None]) & (query_seg[:, None] == key_seg[None, :])
    distance = jnp.maximum(query_pos[:, None] - key_pos[None, :], 0)
    bucket_ids = jnp.arange(rel_table.shape[0], dtype=jnp.int32)
    range_from = jnp.sum((buckets[None, :] < bucket_ids[:, None]).astype(jnp.int32), axis=1)
    range_to = jnp.sum((buckets[None, :] <= bucket_ids[:, None]).astype(jnp.int32), axis=1)
    grid_onehot = (
        (distance[None] >= range_from[:, None, None]) & (distance[None] < range_to[:, None, None])
    ).astype(jnp.float32)
    rel_bias = bias_table(rel_table, grid_onehot)

    normed_both = rms_scaled(tokens_both.astype(jnp.float32), norm_gains[0]).astype(jnp.bfloat16)
    qkv_both = jnp.dot(normed_both, attn_in_all, preferred_element_type=jnp.float32).astype(
        jnp.bfloat16
    )
    queries_one = qkv_both[:tok_count, :model_width].reshape(tok_count, H, HD)
    keys_one = qkv_both[:, model_width : 2 * model_width].reshape(2 * tok_count, H, HD)
    values_one = qkv_both[:, 2 * model_width :].reshape(2 * tok_count, H, HD)
    context, weights_one = attend_forward(queries_one, keys_one, values_one, rel_bias, allowed)
    context_one = context.reshape(tok_count, model_width)
    hidden_one = tok_float + jnp.dot(context_one, attn_out_all, preferred_element_type=jnp.float32)
    normed_two = rms_scaled(hidden_one, norm_gains[1]).astype(jnp.bfloat16)
    queries_two = (
        jnp.dot(normed_two, cross_query_all, preferred_element_type=jnp.float32)
        .astype(jnp.bfloat16)
        .reshape(tok_count, H, HD)
    )
    keyval_two = jnp.dot(enc_both, cross_kv_all, preferred_element_type=jnp.float32).astype(
        jnp.bfloat16
    )
    keys_two = keyval_two[:, :model_width].reshape(2 * enc_count, H, HD)
    values_two = keyval_two[:, model_width:].reshape(2 * enc_count, H, HD)
    context, weights_two = attend_forward(queries_two, keys_two, values_two, None, None)
    context_two = context.reshape(tok_count, model_width)
    hidden_two = hidden_one + jnp.dot(
        context_two, cross_out_all, preferred_element_type=jnp.float32
    )
    normed_three = rms_scaled(hidden_two, norm_gains[2]).astype(jnp.bfloat16)
    pre_act = jnp.dot(normed_three, ff_in_all, preferred_element_type=jnp.float32)
    gate_act = pre_act[:, :FF]
    upward = pre_act[:, FF:]
    mixed_act = gated(gate_act, upward).astype(jnp.bfloat16)
    layer_out = hidden_two + jnp.einsum(
        "tf,df->td", mixed_act, ff_out_all, preferred_element_type=jnp.float32
    )
    grad_out = cotangent[0].astype(jnp.float32)
    grad_branch = cotangent[0]
    grad_mixed = jnp.einsum(
        "td,df->tf", grad_branch, ff_out_all, preferred_element_type=jnp.float32
    )
    gate_value, gate_pull = jax.vjp(gated, gate_act, upward)
    grad_gate, grad_up = gate_pull(grad_mixed)
    grad_gate = grad_gate.astype(jnp.bfloat16)
    grad_up = grad_up.astype(jnp.bfloat16)
    wave = HalvingSum(
        [
            outer_rows(grad_branch, mixed_act),
            outer_rows(normed_three, grad_gate),
            outer_rows(normed_three, grad_up),
        ],
        devices,
        index,
        never,
    )
    grad_pre = after(never, jnp.concatenate([grad_gate, grad_up], 1), wave.sent)
    wave.exchange()
    grad_normed = jnp.einsum("tk,ck->tc", grad_pre, ff_in_all, preferred_element_type=jnp.float32)
    norm_value, norm_pull = jax.vjp(rms_scaled, hidden_two, norm_gains[2])
    grad_resid, gain_three = norm_pull(grad_normed)
    grad_hidden_two = grad_out + grad_resid
    grad_branch_two = after(never, grad_hidden_two.astype(jnp.bfloat16), wave.sent)
    wave.exchange()
    grad_context_two = jnp.einsum(
        "tk,ck->tc", grad_branch_two, cross_out_all, preferred_element_type=jnp.float32
    )
    grad_context_two = grad_context_two.astype(jnp.bfloat16).reshape(tok_count, H, HD)
    grad_queries, grad_keys, grad_values, grad_scores = attend_backward(
        queries_two, keys_two, values_two, weights_two, grad_context_two
    )
    grad_kv_two = jnp.concatenate(
        [
            grad_keys.reshape(2 * enc_count, model_width),
            grad_values.reshape(2 * enc_count, model_width),
        ],
        1,
    )
    kv_two_low = grad_kv_two.astype(jnp.bfloat16)
    cross_grads = jnp.concatenate(
        [outer_rows(enc_both, kv_two_low), outer_rows(context_two, grad_branch_two)], 1
    )
    grad_kv_local = (
        grad_kv_two[:enc_count]
        + swap_bit(kv_two_low[enc_count:], 0, devices).astype(jnp.float32)
    ).astype(jnp.bfloat16)
    grad_queries_two = grad_queries.reshape(tok_count, model_width).astype(jnp.bfloat16)
    grad_queries_two = after(never, grad_queries_two, wave.sent)
    wave.exchange()
    encoder_grad = jnp.einsum(
        "tk,ck->tc", grad_kv_local, cross_kv_all, preferred_element_type=jnp.float32
    )
    grad_normed = jnp.einsum(
        "tk,ck->tc", grad_queries_two, cross_query_all, preferred_element_type=jnp.float32
    )
    norm_value, norm_pull = jax.vjp(rms_scaled, hidden_one, norm_gains[1])
    grad_resid, gain_two = norm_pull(grad_normed)
    grad_hidden_one = grad_hidden_two + grad_resid
    grad_branch_one = grad_hidden_one.astype(jnp.bfloat16)
    middle_grads = jnp.concatenate(
        [outer_rows(normed_two, grad_queries_two), outer_rows(context_one, grad_branch_one)], 1
    )
    grad_context_one = jnp.einsum(
        "tk,ck->tc", grad_branch_one, attn_out_all, preferred_element_type=jnp.float32
    )
    grad_context_one = after(never, grad_context_one.astype(jnp.bfloat16), wave.sent)
    grad_context_one = grad_context_one.reshape(tok_count, H, HD)
    wave.exchange()
    grad_queries, grad_keys, grad_values, grad_scores = attend_backward(
        queries_one, keys_one, values_one, weights_one, grad_context_one
    )
    grad_keys = grad_keys.reshape(2 * tok_count, model_width)
    grad_values = grad_values.reshape(2 * tok_count, model_width)
    keys_low = grad_keys.astype(jnp.bfloat16)
    values_low = grad_values.astype(jnp.bfloat16)
    grad_queries_one = grad_queries.reshape(tok_count, model_width).astype(jnp.bfloat16)
    in_grads = jnp.concatenate(
        [
            outer_rows(normed_both[:tok_count], grad_queries_one),
            outer_rows(normed_both, jnp.concatenate([keys_low, values_low], 1)),
        ],
        1,
    )
    while wave.at < bits:
        wave.exchange()
    ff_out_grad, gate_grad, up_grad = wave.groups
    other_part = swap_bit(
        jnp.concatenate([keys_low[tok_count:], values_low[tok_count:]], 1), 0, devices
    ).astype(jnp.float32)
    grad_kv_own = (
        jnp.concatenate([grad_keys[:tok_count], grad_values[:tok_count]], 1) + other_part
    ).astype(jnp.bfloat16)
    table_grad = jnp.einsum(
        "hij,bij->bh", grad_scores.astype(jnp.float32), grid_onehot, precision=lax.Precision.HIGHEST
    )
    grad_qkv = jnp.concatenate([grad_queries_one, grad_kv_own], 1)
    grad_normed = jnp.einsum("tk,ck->tc", grad_qkv, attn_in_all, preferred_element_type=jnp.float32)
    norm_value, norm_pull = jax.vjp(rms_scaled, tok_float, norm_gains[0])
    grad_resid, gain_one = norm_pull(grad_normed)
    tokens_grad = grad_hidden_one + grad_resid
    small = jnp.concatenate([gain_one, gain_two, gain_three, table_grad.reshape(-1)])
    wave = HalvingSum([in_grads, cross_grads, middle_grads], devices, index, never, small)
    for at in range(bits):
        wave.exchange()
    in_grads, cross_grads, middle_grads = wave.groups
    small = wave.whole
    return (
        layer_out.astype(jnp.bfloat16)[None],
        tokens_grad[None],
        encoder_grad[None],
        small[: 3 * model_width].reshape(3, model_width),
        small[3 * model_width :].reshape(rel_table.shape),
        in_grads,
        middle_grads[:, model_width:],
        middle_grads[:, :model_width],
        cross_grads[:, : 2 * model_width],
        cross_grads[:, 2 * model_width :],
        jnp.concatenate([gate_grad, up_grad], 1),
        ff_out_grad,
    )


def solution(mesh):
    return jax.shard_map(
        functools.partial(local, mesh.devices.size),
        mesh=mesh,
        in_specs=(
            P("dp", "seq", None),
            P("dp", None),
            P(),
            P("dp", "seq", None),
            P(),
            P(),
            P(("dp", "seq"), None),
            P(("dp", "seq"), None),
            P(("dp", "seq"), None),
            P(("dp", "seq"), None),
            P(("dp", "seq"), None),
            P(("dp", "seq"), None),
            P(("dp", "seq"), None),
            P("dp", "seq", None),
        ),
        out_specs=(
            P("dp", "seq", None),
            P("dp", "seq", None),
            P("dp", "seq", None),
            P(),
            P(),
            P(("dp", "seq"), None),
            P(("dp", "seq"), None),
            P(("dp", "seq"), None),
            P(("dp", "seq"), None),
            P(("dp", "seq"), None),
            P(("dp", "seq"), None),
            P(("dp", "seq"), None),
        ),
        check_vma=False,
    )
```

```python
import functools

import jax
import jax.numpy as jnp
from jax import lax
from jax.sharding import PartitionSpec as P

H = 12
HD = 64
FF = 2048


epsilon = 1e-06
masked_value = -1000000000.0


def rms_scaled(values, gain_row):
    return (
        values * lax.rsqrt(jnp.mean(values * values, axis=-1, keepdims=True) + epsilon) * gain_row
    )


def gelu_tanh(values):
    return (
        0.5
        * values
        * (1.0 + jnp.tanh(0.7978845608028654 * (values + 0.044715 * values * values * values)))
    )


def gated(gate_act, upward):
    return gelu_tanh(gate_act) * upward


def bias_table(table_in, grid_onehot):
    return jnp.einsum("bij,bh->hij", grid_onehot, table_in, precision=lax.Precision.HIGHEST)


def attend_forward(queries, key_rows, values, rel_bias, allowed):
    scores = jnp.einsum("rhd,shd->hrs", queries, key_rows, preferred_element_type=jnp.float32)
    if rel_bias is not None:
        scores = jnp.where(allowed[None], scores + rel_bias, masked_value)
    row_top = jnp.max(scores, axis=2, keepdims=True)
    exponent = jnp.exp(scores - row_top)
    row_total = jnp.sum(exponent, axis=2, keepdims=True)
    weights_full = exponent / row_total
    context = jnp.einsum(
        "hrs,shd->rhd",
        weights_full.astype(jnp.bfloat16),
        values,
        preferred_element_type=jnp.float32,
    )
    return (context.astype(jnp.bfloat16), weights_full)


def attend_backward(queries, key_rows, values, weights_full, grad_context):
    weights_low = weights_full.astype(jnp.bfloat16)
    grad_values = jnp.einsum(
        "hrs,rhd->shd", weights_low, grad_context, preferred_element_type=jnp.float32
    )
    grad_weights = jnp.einsum(
        "rhd,shd->hrs", grad_context, values, preferred_element_type=jnp.float32
    )
    row_dot = jnp.sum(grad_weights * weights_full, axis=2, keepdims=True)
    grad_scores = (weights_full * (grad_weights - row_dot)).astype(jnp.bfloat16)
    grad_queries = jnp.einsum(
        "hrs,shd->rhd", grad_scores, key_rows, preferred_element_type=jnp.float32
    )
    grad_keys = jnp.einsum("hrs,rhd->shd", grad_scores, queries, preferred_element_type=jnp.float32)
    return (grad_queries, grad_keys, grad_values, grad_scores)


def outer_rows(left, right):
    return jnp.einsum("tc,tk->ck", left, right, preferred_element_type=jnp.float32).astype(
        jnp.bfloat16
    )


axes = ("dp", "seq")


def swap_bit(values, bit, devices):
    return lax.ppermute(values, axes, [(at, at ^ (1 << bit)) for at in range(devices)])


def bit_order(bits, turn):
    rest = [0] + list(range(2, bits))
    turn = turn % len(rest)
    return [1] + rest[turn:] + rest[:turn]


def scatter_sum(values, order, devices, index):
    bits = len(order)
    values = values.reshape((2,) * bits + (values.shape[0] // devices, values.shape[1]))
    left = list(range(bits - 1, -1, -1))
    for bit in order:
        place = left.index(bit)
        mine = (index >> bit) & 1
        kept = lax.dynamic_index_in_dim(values, mine, place, keepdims=False)
        sent = lax.dynamic_index_in_dim(values, 1 - mine, place, keepdims=False)
        total = kept.astype(jnp.float32) + swap_bit(sent, bit, devices).astype(jnp.float32)
        left.remove(bit)
        values = total.astype(jnp.bfloat16) if left else total
    return values


def after(never, values, other):
    return jnp.where(never, other[0, 0].astype(values.dtype), values)


def full_sum(values, bits, devices):
    for bit in range(bits):
        values = values + swap_bit(values, bit, devices)
    return values


def local(
    devices,
    tokens,
    segment_ids,
    buckets,
    encoder,
    norm_gains,
    rel_table,
    attn_in,
    attn_out,
    cross_query,
    cross_kv,
    cross_out,
    ff_in,
    ff_out,
    cotangent,
):
    bits = devices.bit_length() - 1
    tok_count = tokens.shape[1]
    model_width = tokens.shape[2]
    enc_count = encoder.shape[1]
    my_seq = lax.axis_index("seq")
    index = lax.axis_index("dp") * 2 + my_seq

    never = segment_ids[0, 0] < 0

    def scattered(values, turn):
        return scatter_sum(values, bit_order(bits, turn), devices, index)

    shards = (attn_in, attn_out, cross_query, cross_kv, cross_out, ff_in, ff_out)
    gathered = lax.all_gather(jnp.concatenate(shards, 1), axes, axis=0, tiled=True)
    whole = []
    column = 0
    for shard in shards:
        whole.append(gathered[:, column : column + shard.shape[1]])
        column += shard.shape[1]
    (
        attn_in_all,
        attn_out_all,
        cross_query_all,
        cross_kv_all,
        cross_out_all,
        ff_in_all,
        ff_out_all,
    ) = whole

    tokens_both = jnp.concatenate([tokens[0], swap_bit(tokens[0], 0, devices)], 0)
    enc_both = jnp.concatenate([encoder[0], swap_bit(encoder[0], 0, devices)], 0)
    tok_float = tokens[0].astype(jnp.float32)
    segments = segment_ids[0]
    own_start = my_seq * tok_count
    other_start = (1 - my_seq) * tok_count
    steps = jnp.arange(tok_count, dtype=jnp.int32)
    query_pos = own_start + steps
    key_pos = jnp.concatenate([query_pos, other_start + steps])
    query_seg = lax.dynamic_slice_in_dim(segments, own_start, tok_count)
    key_seg = jnp.concatenate(
        [query_seg, lax.dynamic_slice_in_dim(segments, other_start, tok_count)]
    )
    allowed = (key_pos[None, :] <= query_pos[:, None]) & (query_seg[:, None] == key_seg[None, :])
    distance = jnp.maximum(query_pos[:, None] - key_pos[None, :], 0)
    bucket_ids = jnp.arange(rel_table.shape[0], dtype=jnp.int32)
    range_from = jnp.sum((buckets[None, :] < bucket_ids[:, None]).astype(jnp.int32), axis=1)
    range_to = jnp.sum((buckets[None, :] <= bucket_ids[:, None]).astype(jnp.int32), axis=1)
    grid_onehot = (
        (distance[None] >= range_from[:, None, None]) & (distance[None] < range_to[:, None, None])
    ).astype(jnp.float32)
    rel_bias = bias_table(rel_table, grid_onehot)

    normed_both = rms_scaled(tokens_both.astype(jnp.float32), norm_gains[0]).astype(jnp.bfloat16)
    qkv_both = jnp.dot(normed_both, attn_in_all, preferred_element_type=jnp.float32).astype(
        jnp.bfloat16
    )
    queries_one = qkv_both[:tok_count, :model_width].reshape(tok_count, H, HD)
    keys_one = qkv_both[:, model_width : 2 * model_width].reshape(2 * tok_count, H, HD)
    values_one = qkv_both[:, 2 * model_width :].reshape(2 * tok_count, H, HD)
    context, weights_one = attend_forward(queries_one, keys_one, values_one, rel_bias, allowed)
    context_one = context.reshape(tok_count, model_width)
    hidden_one = tok_float + jnp.dot(context_one, attn_out_all, preferred_element_type=jnp.float32)
    normed_two = rms_scaled(hidden_one, norm_gains[1]).astype(jnp.bfloat16)
    queries_two = (
        jnp.dot(normed_two, cross_query_all, preferred_element_type=jnp.float32)
        .astype(jnp.bfloat16)
        .reshape(tok_count, H, HD)
    )
    keyval_two = jnp.dot(enc_both, cross_kv_all, preferred_element_type=jnp.float32).astype(
        jnp.bfloat16
    )
    keys_two = keyval_two[:, :model_width].reshape(2 * enc_count, H, HD)
    values_two = keyval_two[:, model_width:].reshape(2 * enc_count, H, HD)
    context, weights_two = attend_forward(queries_two, keys_two, values_two, None, None)
    context_two = context.reshape(tok_count, model_width)
    hidden_two = hidden_one + jnp.dot(
        context_two, cross_out_all, preferred_element_type=jnp.float32
    )
    normed_three = rms_scaled(hidden_two, norm_gains[2]).astype(jnp.bfloat16)
    pre_act = jnp.dot(normed_three, ff_in_all, preferred_element_type=jnp.float32)
    gate_act = pre_act[:, :FF]
    upward = pre_act[:, FF:]
    mixed_act = gated(gate_act, upward).astype(jnp.bfloat16)
    layer_out = hidden_two + jnp.einsum(
        "tf,df->td", mixed_act, ff_out_all, preferred_element_type=jnp.float32
    )
    grad_out = cotangent[0].astype(jnp.float32)
    grad_branch = cotangent[0]
    grad_mixed = jnp.einsum(
        "td,df->tf", grad_branch, ff_out_all, preferred_element_type=jnp.float32
    )
    gate_value, gate_pull = jax.vjp(gated, gate_act, upward)
    grad_gate, grad_up = gate_pull(grad_mixed)
    grad_gate = grad_gate.astype(jnp.bfloat16)
    grad_up = grad_up.astype(jnp.bfloat16)
    grad_pre = jnp.concatenate([grad_gate, grad_up], 1)
    ff_grads = jnp.concatenate(
        [outer_rows(normed_three, grad_pre), outer_rows(grad_branch, mixed_act)], 1
    )
    grad_pre = after(never, grad_pre, ff_grads)
    ff_grads = lax.psum_scatter(ff_grads, axes, scatter_dimension=0, tiled=True)
    ff_grads = ff_grads.astype(jnp.float32)
    grad_normed = jnp.einsum("tk,ck->tc", grad_pre, ff_in_all, preferred_element_type=jnp.float32)
    norm_value, norm_pull = jax.vjp(rms_scaled, hidden_two, norm_gains[2])
    grad_resid, gain_three = norm_pull(grad_normed)
    grad_hidden_two = grad_out + grad_resid
    grad_branch_two = grad_hidden_two.astype(jnp.bfloat16)
    grad_context_two = jnp.einsum(
        "tk,ck->tc", grad_branch_two, cross_out_all, preferred_element_type=jnp.float32
    )
    grad_context_two = grad_context_two.astype(jnp.bfloat16).reshape(tok_count, H, HD)
    grad_queries, grad_keys, grad_values, grad_scores = attend_backward(
        queries_two, keys_two, values_two, weights_two, grad_context_two
    )
    grad_kv_two = jnp.concatenate(
        [
            grad_keys.reshape(2 * enc_count, model_width),
            grad_values.reshape(2 * enc_count, model_width),
        ],
        1,
    )
    kv_two_low = grad_kv_two.astype(jnp.bfloat16)
    cross_grads = scattered(
        jnp.concatenate(
            [outer_rows(enc_both, kv_two_low), outer_rows(context_two, grad_branch_two)], 1
        ),
        1,
    )
    grad_kv_local = (
        grad_kv_two[:enc_count]
        + swap_bit(kv_two_low[enc_count:], 0, devices).astype(jnp.float32)
    ).astype(jnp.bfloat16)
    grad_queries_two = grad_queries.reshape(tok_count, model_width).astype(jnp.bfloat16)
    encoder_grad = jnp.einsum(
        "tk,ck->tc", grad_kv_local, cross_kv_all, preferred_element_type=jnp.float32
    )
    grad_normed = jnp.einsum(
        "tk,ck->tc", grad_queries_two, cross_query_all, preferred_element_type=jnp.float32
    )
    norm_value, norm_pull = jax.vjp(rms_scaled, hidden_one, norm_gains[1])
    grad_resid, gain_two = norm_pull(grad_normed)
    grad_hidden_one = grad_hidden_two + grad_resid
    grad_branch_one = grad_hidden_one.astype(jnp.bfloat16)
    middle_grads = scattered(
        jnp.concatenate(
            [outer_rows(normed_two, grad_queries_two), outer_rows(context_one, grad_branch_one)], 1
        ),
        2,
    )
    grad_context_one = jnp.einsum(
        "tk,ck->tc", grad_branch_one, attn_out_all, preferred_element_type=jnp.float32
    )
    grad_context_one = grad_context_one.astype(jnp.bfloat16).reshape(tok_count, H, HD)
    grad_queries, grad_keys, grad_values, grad_scores = attend_backward(
        queries_one, keys_one, values_one, weights_one, grad_context_one
    )
    grad_keys = grad_keys.reshape(2 * tok_count, model_width)
    grad_values = grad_values.reshape(2 * tok_count, model_width)
    keys_low = grad_keys.astype(jnp.bfloat16)
    values_low = grad_values.astype(jnp.bfloat16)
    grad_queries_one = grad_queries.reshape(tok_count, model_width).astype(jnp.bfloat16)
    in_grads = scattered(
        jnp.concatenate(
            [
                outer_rows(normed_both[:tok_count], grad_queries_one),
                outer_rows(normed_both, jnp.concatenate([keys_low, values_low], 1)),
            ],
            1,
        ),
        0,
    )
    other_part = swap_bit(
        jnp.concatenate([keys_low[tok_count:], values_low[tok_count:]], 1), 0, devices
    ).astype(jnp.float32)
    grad_kv_own = (
        jnp.concatenate([grad_keys[:tok_count], grad_values[:tok_count]], 1) + other_part
    ).astype(jnp.bfloat16)
    table_grad = jnp.einsum(
        "hij,bij->bh", grad_scores.astype(jnp.float32), grid_onehot, precision=lax.Precision.HIGHEST
    )
    grad_qkv = jnp.concatenate([grad_queries_one, grad_kv_own], 1)
    grad_normed = jnp.einsum("tk,ck->tc", grad_qkv, attn_in_all, preferred_element_type=jnp.float32)
    norm_value, norm_pull = jax.vjp(rms_scaled, tok_float, norm_gains[0])
    grad_resid, gain_one = norm_pull(grad_normed)
    tokens_grad = grad_hidden_one + grad_resid
    small = jnp.concatenate([gain_one, gain_two, gain_three, table_grad.reshape(-1)])
    small = full_sum(small, bits, devices)
    return (
        layer_out.astype(jnp.bfloat16)[None],
        tokens_grad[None],
        encoder_grad[None],
        small[: 3 * model_width].reshape(3, model_width),
        small[3 * model_width :].reshape(rel_table.shape),
        in_grads,
        middle_grads[:, model_width:],
        middle_grads[:, :model_width],
        cross_grads[:, : 2 * model_width],
        cross_grads[:, 2 * model_width :],
        ff_grads[:, : 2 * FF],
        ff_grads[:, 2 * FF :],
    )


def solution(mesh):
    return jax.shard_map(
        functools.partial(local, mesh.devices.size),
        mesh=mesh,
        in_specs=(
            P("dp", "seq", None),
            P("dp", None),
            P(),
            P("dp", "seq", None),
            P(),
            P(),
            P(("dp", "seq"), None),
            P(("dp", "seq"), None),
            P(("dp", "seq"), None),
            P(("dp", "seq"), None),
            P(("dp", "seq"), None),
            P(("dp", "seq"), None),
            P(("dp", "seq"), None),
            P("dp", "seq", None),
        ),
        out_specs=(
            P("dp", "seq", None),
            P("dp", "seq", None),
            P("dp", "seq", None),
            P(),
            P(),
            P(("dp", "seq"), None),
            P(("dp", "seq"), None),
            P(("dp", "seq"), None),
            P(("dp", "seq"), None),
            P(("dp", "seq"), None),
            P(("dp", "seq"), None),
            P(("dp", "seq"), None),
        ),
        check_vma=False,
    )
```
